32 devices in a mesh: groups: 2 (over y), layer: 4 (over z), dp: 2 (over x), chan: 2 (over core).
Axes of the slice: x: 2, y: 2, z: 4, core: 2. Of those that a mesh axis runs over, the one named last changes fastest.
Arguments:
- activations: bfloat16 [4, 4, 32, 16, 16, 128], P('layer', None, ('groups', 'dp', 'chan')), parts along dimension 2, may hold values from -0.94921875 to 0.94921875
- weights: bfloat16 [4, 4, 9, 128, 128], P('layer'), may hold values from -0.1875 to 0.1875
- guesses: bfloat16 [4, 32, 16, 16, 128], P('layer', ('groups', 'dp', 'chan')), parts along dimension 1, may hold values from -6 to 6
- terminal: bfloat16 [32, 16, 16, 128], P(('groups', 'dp', 'chan')), parts along dimension 0, may hold values from -6 to 6
- coarse_rates: float32 [4, 128], P('layer'), may hold values from 0.0074 to 1, as said below
- block_layers: int32 [4], P('layer'), may hold values from 1 to 4, 12 in all
Outputs:
- corrected: bfloat16 [4, 32, 16, 16, 128], P('layer', ('groups', 'dp', 'chan')), parts along dimension 1
- kernel_grads: bfloat16 [8, 4, 9, 128, 128], P(('groups', 'layer')), parts along dimension 0
The draws below stay inside these ranges and needn't reach their ends.
There are 2 independent parts, one for each index of `groups`. The reference program is written for one: setup_inputs(seed, part) draws one part's arguments, and reference() takes and returns one part's arrays. A program takes and returns all parts, laid end to end along the dimension named above; an argument that names none is the same for every part. Nothing has to cross between parts.
Inputs may be any that keep to these rules, and one draw needn't show every extreme that they name: `block_layers`: every block holds at least one layer and some block holds exactly 4; the counts sum to 12. `coarse_rates`: strictly positive.
All inputs are finite; a program needn't handle non-finite values.
Results may differ from the reference program's by a relative error of at most 0.0055.
Values may be sent and summed in bfloat16 or wider, within the bound.
A program may use at most 64 MiB of HBM per device.

```python
import math
import jax
import jax.numpy as jnp
import numpy as np
from jax import lax

C = 128
SIDE = 16
MMAX = 4
NB = 4
LAYERS = 12
BATCH = 16


def draw_coarse_rates(key, part):
    first, second, third, fourth = jax.random.split(key, 4)
    forget = jnp.exp(jax.random.uniform(first, (C,), jnp.float32, math.log(0.3 / NB), math.log(3.0)))
    jitter = jax.random.uniform(second, (NB, C), jnp.float32, 0.5, 1.4)
    bursty = jax.random.uniform(third, (NB, C), jnp.float32) < 2.0 / NB
    loss = jax.random.uniform(fourth, (NB, C), jnp.float32, 0.5, 0.8)
    factor = jnp.where(bursty, loss, 1.0)
    return (jnp.exp(-forget[None, :] * jitter) * factor).astype(jnp.float32)


def shard_levels(own_key, extent, shards, smallest, top_value):
    def one(dim, shards_of):
        draws = jax.random.uniform(jax.random.fold_in(jax.random.fold_in(own_key, 6), dim), (shards_of,), jnp.float32, smallest / len(shards), top_value / len(shards))
        return jnp.repeat(jnp.exp(draws), extent[dim] // shards_of).reshape((-1,) + (1,) * (len(extent) - dim - 1))

    level = one(*shards[0])
    for cut in shards[1:]:
        level = level * one(*cut)
    return level


def profile(count, total, reach, lean):
    portions = [(1 << 20) // math.isqrt(standing ** lean) + 1 for standing in range(2, count + 1)]
    rest, given = total - reach - (count - 1), [1] * (count - 1)
    while rest > 0:
        free = [i for i in range(count - 1) if given[i] < reach]
        whole, budget = sum([portions[i] for i in free]), rest
        for i in free:
            addition = min(reach - given[i], max(1, budget * portions[i] // whole), rest)
            given[i] = given[i] + addition
            rest = rest - addition
    return np.array([reach] + given)


def uneven(stream_key, amount, total, most, lean):
    if amount == 2:
        one = jax.random.randint(stream_key, (), max(1, total - most), min(most, total - 1) + 1)
        return jnp.stack([one, total - one])
    lengths = jnp.asarray(profile(amount, total, most, lean), jnp.int32)
    pairs = (amount - 1) // 2
    giver, sink = lengths[1:1 + 2 * pairs:2], lengths[2:2 + 2 * pairs:2]
    slack = jnp.minimum(giver - 1, most - sink)
    passed = jax.random.randint(jax.random.fold_in(stream_key, 1), (pairs,), 0, 1 << 20) % (slack + 1)
    lengths = lengths.at[1:1 + 2 * pairs:2].set(giver - passed).at[2:2 + 2 * pairs:2].set(sink + passed)
    return lengths[jax.random.permutation(jax.random.fold_in(stream_key, 2), amount)]


def noise(stream_key, dims, width, most, shards=(), kind=jnp.bfloat16):
    result = width * jax.random.normal(stream_key, dims, jnp.float32)
    if shards:
        result = result * shard_levels(stream_key, dims, shards, -0.22, 0.18)
    return jnp.clip(result, -most, most).astype(kind)


def setup_inputs(seed: int = 0, part: int = 0) -> dict:
    arg_keys = jax.random.split(jax.random.key(seed), 7)
    part_keys = jax.random.split(jax.random.fold_in(arg_keys[6], part), 7)
    activations = jnp.clip(jax.random.uniform(part_keys[0], (NB, MMAX, BATCH, SIDE, SIDE, C), jnp.float32, -0.94921875, 0.94921875) * shard_levels(part_keys[0], (NB, MMAX, BATCH, SIDE, SIDE, C), ((0, 4), (2, 4)), -0.4, 0.0), -0.94921875, 0.94921875).astype(jnp.bfloat16)
    weights = noise(arg_keys[1], (NB, MMAX, 9, C, C), (9 * C) ** -0.5, 0.1875, ((0, 4),))
    guesses = noise(part_keys[2], (NB, BATCH, SIDE, SIDE, C), 1.0, 6.0, ((0, 4), (1, 4)))
    terminal = noise(part_keys[3], (BATCH, SIDE, SIDE, C), 1.0, 6.0, ((0, 4),))
    coarse_rates = draw_coarse_rates(jax.random.fold_in(arg_keys[6], 71), part)
    block_layers = uneven(arg_keys[5], NB, LAYERS, MMAX, 2).astype(jnp.int32)
    return {"activations": activations, "weights": weights, "guesses": guesses, "terminal": terminal, "coarse_rates": coarse_rates, "block_layers": block_layers}


step_size = 0.25
OFFSETS = [(row_off, col_off) for row_off in (-1, 0, 1) for col_off in (-1, 0, 1)]

def adjoint_step(adjoint, activation, kernel):
    map_side = adjoint.shape[1]
    rounded = adjoint.astype(jnp.bfloat16)
    padded = jnp.pad(rounded, ((0, 0), (1, 1), (1, 1), (0, 0)))
    summed = jnp.zeros(adjoint.shape, jnp.float32)
    for index, (row_off, col_off) in enumerate(OFFSETS):
        sliced = padded[:, 1 - row_off:1 - row_off + map_side, 1 - col_off:1 - col_off + map_side, :]
        summed = summed + jnp.dot(sliced, kernel[index].T, preferred_element_type=jnp.float32)
    act_float = activation.astype(jnp.float32)
    return (adjoint + step_size * (1.0 - act_float * act_float) * summed, rounded)

def kernel_grad(activation, rounded):
    map_side = rounded.shape[1]
    padded = jnp.pad(activation, ((0, 0), (1, 1), (1, 1), (0, 0)))
    pieces = []
    for row_off, col_off in OFFSETS:
        sliced = padded[:, 1 + row_off:1 + row_off + map_side, 1 + col_off:1 + col_off + map_side, :]
        pieces.append(lax.dot_general(sliced, rounded, (((0, 1, 2), (0, 1, 2)), ((), ())), preferred_element_type=jnp.float32))
    return step_size * jnp.stack(pieces)

def relax(above, acts_block, kernels_block, layer_count, with_grads):
    adjoint = above
    slot_list = [None] * MMAX
    for slot in reversed(range(MMAX)):
        stepped, rounded = adjoint_step(adjoint, acts_block[slot], kernels_block[slot])
        active = slot < layer_count
        if with_grads:
            slot_grad = kernel_grad(acts_block[slot], rounded)
            slot_list[slot] = jnp.where(active, slot_grad, jnp.zeros_like(slot_grad))
        adjoint = jnp.where(active, stepped, adjoint)
    return (adjoint, slot_list)

def reference(activations, weights, guesses, terminal, coarse_rates, block_layers):
    end_state = terminal.astype(jnp.float32)
    residuals = []
    for block in range(NB):
        above = end_state if block == NB - 1 else guesses[block + 1].astype(jnp.float32)
        propagated, _ = relax(above, activations[block], weights[block], block_layers[block], False)
        residuals.append(propagated - guesses[block].astype(jnp.float32))
    corrected = [None] * NB
    following = jnp.zeros(end_state.shape, jnp.float32)
    for block in reversed(range(NB)):
        correction = residuals[block] + coarse_rates[block] * following
        corrected[block] = (guesses[block].astype(jnp.float32) + correction).astype(jnp.bfloat16)
        following = correction
    grads = []
    for block in range(NB):
        above = end_state if block == NB - 1 else corrected[block + 1].astype(jnp.float32)
        _, slot_list = relax(above, activations[block], weights[block], block_layers[block], True)
        grads.append(jnp.stack(slot_list))
    return (jnp.stack(corrected), jnp.stack(grads).astype(jnp.bfloat16))
```

```python
import functools

import jax
import jax.numpy as jnp
from jax import lax
from jax.experimental import pallas as pl
from jax.experimental.pallas import tpu as pltpu
from jax.sharding import PartitionSpec as P

STEP = 0.25
MESH = pl.DeviceIdType.MESH


def kernel(
    sizes,
    acts_hbm, w_hbm, guess_hbm, term_hbm, rates_ref, count_ref,
    corr_hbm, grads_hbm,
    acts, w, wt, at, gbuf, rbuf, cbuf, state, shifts, grad, part, xbuf, fin,
    local_sem, gsend, grecv, csend, crecv, psend, precv, xsend, xrecv, fsend, frecv, out_sem,
):
    layers, dps, chans = sizes
    slots, samples, side, _, chan = acts.shape
    cells = side * side
    l, d, c = lax.axis_index("layer"), lax.axis_index("dp"), lax.axis_index("chan")
    has_next, has_prev = l < layers - 1, l > 0
    half = grad.shape[2]

    loads = [
        pltpu.make_async_copy(w_hbm, w, local_sem.at[0]),
        pltpu.make_async_copy(acts_hbm, acts, local_sem.at[1]),
    ]
    for load in loads:
        load.start()
    load_term = pltpu.make_async_copy(term_hbm, gbuf, local_sem.at[2])

    @pl.when(jnp.logical_not(has_next))
    def _():
        load_term.start()

    barrier = pltpu.get_barrier_semaphore()

    @pl.when(has_prev)
    def _():
        pl.semaphore_signal(barrier, inc=1, device_id={"layer": l - 1}, device_id_type=MESH)

    @pl.when(has_next)
    def _():
        pl.semaphore_signal(barrier, inc=1, device_id={"layer": l + 1}, device_id_type=MESH)

    pl.semaphore_signal(barrier, inc=1, device_id={"chan": 1 - c}, device_id_type=MESH)
    for k in range(1, dps):
        pl.semaphore_signal(
            barrier, inc=1, device_id={"dp": lax.rem(d + k, dps)}, device_id_type=MESH
        )
    along = (l + layers - 1) // layers + (2 * layers - 2 - l) // layers
    pl.semaphore_wait(barrier, dps + along)

    def guess_copy(n):
        return pltpu.make_async_remote_copy(
            src_ref=guess_hbm.at[n], dst_ref=gbuf.at[n],
            send_sem=gsend.at[n], recv_sem=grecv.at[n],
            device_id={"layer": l - 1}, device_id_type=MESH,
        )

    def corr_copy(n):
        return pltpu.make_async_remote_copy(
            src_ref=cbuf.at[n], dst_ref=rbuf.at[n],
            send_sem=csend.at[n], recv_sem=crecv.at[n],
            device_id={"layer": l - 1}, device_id_type=MESH,
        )

    @pl.when(has_prev)
    def _():
        for n in range(samples):
            guess_copy(n).start()

    shifts[:, 0] = jnp.zeros((samples,) + shifts.shape[2:], shifts.dtype)
    shifts[:, side + 1] = jnp.zeros((samples,) + shifts.shape[2:], shifts.dtype)
    for load in loads:
        load.wait()
    for slot in range(slots):
        for tap in range(9):
            wt[slot, tap * chan:(tap + 1) * chan] = w[slot, tap].T
    for slot in range(slots):
        for n in range(samples):
            at[slot, :, n * cells:(n + 1) * cells] = acts[slot, n].reshape(cells, chan).T

    count = count_ref[0]
    coefs = [jnp.where(slot < count, STEP, 0.0).astype(jnp.float32) for slot in range(slots)]

    def spread(lo, number):
        rows = number * cells
        value = state[lo * cells:lo * cells + rows]
        place = lax.broadcasted_iota(jnp.int32, (rows, chan), 0) % side
        right = jnp.where(place == side - 1, 0.0, pltpu.roll(value, rows - 1, 0))
        left = jnp.where(place == 0, 0.0, pltpu.roll(value, 1, 0))
        for at_lane, piece in enumerate((right, value, left)):
            shifts[lo:lo + number, 1:side + 1, :, at_lane * chan:(at_lane + 1) * chan] = (
                piece.astype(jnp.bfloat16).reshape(number, side, side, chan)
            )

    def moved(lo, number, row):
        first = 2 - row
        return shifts[lo:lo + number, first:first + side].reshape(number * cells, 3 * chan)

    def advance(lo, number, slot):
        rows = slice(lo * cells, (lo + number) * cells)
        back = None
        for row in range(3):
            term = jnp.dot(
                moved(lo, number, row), wt[slot, row * 3 * chan:(row + 1) * 3 * chan],
                preferred_element_type=jnp.float32,
            )
            back = term if back is None else back + term
        a = acts[slot, lo:lo + number].reshape(number * cells, chan).astype(jnp.float32)
        state[rows] = state[rows] + coefs[slot] * (1.0 - a * a) * back

    def gradient(lo, number, slot, add):
        for row in range(3):
            value = coefs[slot] * jnp.dot(
                at[slot, :, lo * cells:(lo + number) * cells], moved(lo, number, row),
                preferred_element_type=jnp.float32,
            )
            for col in range(3):
                start = (row * 3 + col) * chan
                tile = value[:, col * chan:(col + 1) * chan]
                done = 0
                while done < chan:
                    which, place = divmod(start + done, half)
                    size = min(chan - done, half - place)
                    piece = tile[done:done + size]
                    if add:
                        piece = piece + grad[slot, which, place:place + size]
                    grad[slot, which, place:place + size] = piece
                    done += size

    def settle(n):
        @pl.when(jnp.logical_not(has_next))
        def _():
            rbuf[n] = gbuf[n]

        @pl.when(has_next)
        def _():
            corr_copy(n).wait_recv()

        later = rbuf[n].astype(jnp.float32) - gbuf[n].astype(jnp.float32)
        later = later.reshape(cells, chan)
        whole = prop_of(n) + rates_ref[...] * later
        cbuf[n] = whole.astype(jnp.bfloat16).reshape(side, side, chan)

        @pl.when(has_prev)
        def _():
            corr_copy(n).start()

    def prop_of(n):
        return state[n * cells:(n + 1) * cells]

    @pl.when(jnp.logical_not(has_next))
    def _():
        load_term.wait()

    behind = layers - 1 - l
    for n in range(samples):
        @pl.when(has_next)
        def _():
            guess_copy(n).wait_recv()

        state[n * cells:(n + 1) * cells] = gbuf[n].astype(jnp.float32).reshape(cells, chan)
        for slot in reversed(range(slots)):
            spread(n, 1)
            advance(n, 1, slot)
        if n < samples - 1:
            for m in range(n + 1):
                @pl.when(behind == n - m)
                def _():
                    settle(m)

    top = slots - 1
    for n in range(samples):
        @pl.when(behind >= samples - 1 - n)
        def _():
            settle(n)

        state[n * cells:(n + 1) * cells] = rbuf[n].astype(jnp.float32).reshape(cells, chan)
        spread(n, 1)
        gradient(n, 1, top, n > 0)
        advance(n, 1, top)

    out_corr = pltpu.make_async_copy(cbuf, corr_hbm, out_sem.at[0, 0])
    out_corr.start()

    def partner_copy(slot):
        return pltpu.make_async_remote_copy(
            src_ref=grad.at[slot, 1 - c], dst_ref=part.at[slot],
            send_sem=psend.at[slot], recv_sem=precv.at[slot],
            device_id={"chan": 1 - c}, device_id_type=MESH,
        )

    def peer_copy(slot, source, target):
        return pltpu.make_async_remote_copy(
            src_ref=xbuf.at[source, slot], dst_ref=xbuf.at[source, slot],
            send_sem=xsend.at[slot, target], recv_sem=xrecv.at[slot, source],
            device_id={"dp": target}, device_id_type=MESH,
        )

    def final_copy(slot, which):
        return pltpu.make_async_remote_copy(
            src_ref=fin.at[slot, which], dst_ref=fin.at[slot, which],
            send_sem=fsend.at[slot], recv_sem=frecv.at[slot],
            device_id={"chan": 1 - c}, device_id_type=MESH,
        )

    def out_copy(slot, which, sem):
        return pltpu.make_async_copy(
            fin.at[slot, which], grads_hbm.at[slot, which], out_sem.at[sem, slot]
        )

    def chip_sum(slot):
        partner_copy(slot).wait_recv()
        xbuf[d, slot] = (grad[slot, c] + part[slot]).astype(jnp.bfloat16)
        for k in range(1, dps):
            peer_copy(slot, d, lax.rem(d + k, dps)).start()

    def finish(slot):
        for k in range(1, dps):
            peer_copy(slot, lax.rem(d + k, dps), lax.rem(d + k, dps)).wait_recv()
        total = xbuf[0, slot].astype(jnp.float32)
        for e in range(1, dps):
            total = total + xbuf[e, slot].astype(jnp.float32)
        fin[slot, c] = total.astype(jnp.bfloat16)
        final_copy(slot, c).start()
        out_copy(slot, c, 1).start()

    def collect(slot):
        final_copy(slot, 1 - c).wait_recv()
        out_copy(slot, 1 - c, 2).start()

    partner_copy(top).start()
    for slot in reversed(range(top)):
        spread(0, samples)
        gradient(0, samples, slot, False)
        partner_copy(slot).start()
        chip_sum(slot + 1)
        if slot:
            advance(0, samples, slot)
    chip_sum(0)
    for slot in reversed(range(slots)):
        finish(slot)
        if slot < top:
            collect(slot + 1)
    collect(0)

    @pl.when(has_prev)
    def _():
        for n in range(samples):
            guess_copy(n).wait_send()
            corr_copy(n).wait_send()

    out_corr.wait()
    for slot in range(slots):
        partner_copy(slot).wait_send()
        for k in range(1, dps):
            peer_copy(slot, d, lax.rem(d + k, dps)).wait_send()
        final_copy(slot, c).wait_send()
        out_copy(slot, c, 1).wait()
        out_copy(slot, 1 - c, 2).wait()


def per_device(sizes, activations, weights, guesses, terminal, coarse_rates, block_layers):
    _, slots, samples, side, _, chan = activations.shape
    taps = weights.shape[2]
    layers, dps, chans = sizes
    half = taps * chan // 2
    cells = side * side
    bf, f32 = jnp.bfloat16, jnp.float32
    anywhere = pl.BlockSpec(memory_space=pl.ANY)
    dma = pltpu.SemaphoreType.DMA
    flops = 2 * samples * cells * chan * chan * taps * slots * 3
    corrected, grads = pl.pallas_call(
        functools.partial(kernel, sizes),
        out_shape=(
            jax.ShapeDtypeStruct((samples, side, side, chan), bf),
            jax.ShapeDtypeStruct((slots, 2, half, chan), bf),
        ),
        in_specs=[anywhere] * 4
        + [pl.BlockSpec(memory_space=pltpu.VMEM), pl.BlockSpec(memory_space=pltpu.SMEM)],
        out_specs=(anywhere, anywhere),
        scratch_shapes=[
            pltpu.VMEM((slots, samples, side, side, chan), bf),
            pltpu.VMEM((slots, taps, chan, chan), bf),
            pltpu.VMEM((slots, taps * chan, chan), bf),
            pltpu.VMEM((slots, chan, samples * cells), bf),
            pltpu.VMEM((samples, side, side, chan), bf),
            pltpu.VMEM((samples, side, side, chan), bf),
            pltpu.VMEM((samples, side, side, chan), bf),
            pltpu.VMEM((samples * cells, chan), f32),
            pltpu.VMEM((samples, side + 2, side, 3 * chan), bf),
            pltpu.VMEM((slots, 2, half, chan), f32),
            pltpu.VMEM((slots, half, chan), f32),
            pltpu.VMEM((dps, slots, half, chan), bf),
            pltpu.VMEM((slots, 2, half, chan), bf),
            dma((3,)),
            dma((samples,)), dma((samples,)), dma((samples,)), dma((samples,)),
            dma((slots,)), dma((slots,)),
            dma((slots, dps)), dma((slots, dps)),
            dma((slots,)), dma((slots,)),
            dma((3, slots)),
        ],
        compiler_params=pltpu.CompilerParams(
            collective_id=0, has_side_effects=True, vmem_limit_bytes=60 * 1024 * 1024
        ),
        cost_estimate=pl.CostEstimate(flops=flops, bytes_accessed=5_000_000, transcendentals=0),
        name="sweep",
    )(activations[0], weights[0], guesses[0], terminal, coarse_rates, block_layers)
    return corrected[None], grads.reshape(1, slots, taps, chan, chan)


def solution(mesh):
    sizes = (mesh.shape["layer"], mesh.shape["dp"], mesh.shape["chan"])
    batch = ("groups", "dp", "chan")
    in_specs = (
        P("layer", None, batch, None, None, None),
        P("layer", None, None, None, None),
        P("layer", batch, None, None, None),
        P(batch, None, None, None),
        P("layer", None),
        P("layer"),
    )
    out_specs = (
        P("layer", batch, None, None, None),
        P(("groups", "layer"), None, None, None, None),
    )
    return jax.shard_map(
        functools.partial(per_device, sizes),
        mesh=mesh, in_specs=in_specs, out_specs=out_specs, check_vma=False,
    )
```

```python
import functools

import jax
import jax.numpy as jnp
from jax import lax
from jax.experimental import pallas as pl
from jax.experimental.pallas import tpu as pltpu
from jax.sharding import PartitionSpec as P

STEP = 0.25
MESH = pl.DeviceIdType.MESH


def kernel(
    sizes,
    acts_hbm, w_hbm, guess_hbm, term_hbm, rates_ref, count_ref,
    corr_hbm, grads_hbm,
    acts, w, wt, at, gbuf, rbuf, kbuf, cbuf, pbuf, kout, own, rnext, state, start, shifts, grad, part, xbuf, fin,
    local_sem, gsend, grecv, csend, crecv, ksend, krecv, rsend, rrecv, psend, precv, xsend, xrecv, fsend, frecv, out_sem,
):
    layers, dps, chans = sizes
    slots, samples, side, _, chan = acts.shape
    cells = side * side
    l, d, c = lax.axis_index("layer"), lax.axis_index("dp"), lax.axis_index("chan")
    has_next, has_prev = l < layers - 1, l > 0
    half = grad.shape[2]
    behind = layers - 1 - l
    odd = lax.rem(behind, 2) == 1
    to_second = odd & (l > 1)
    from_second = odd & (behind > 1)

    loads = [
        pltpu.make_async_copy(w_hbm, w, local_sem.at[0]),
        pltpu.make_async_copy(acts_hbm, acts, local_sem.at[1]),
        pltpu.make_async_copy(guess_hbm, own, local_sem.at[3]),
    ]
    for load in loads:
        load.start()
    load_term = pltpu.make_async_copy(term_hbm, gbuf, local_sem.at[2])

    @pl.when(jnp.logical_not(has_next))
    def _():
        load_term.start()

    barrier = pltpu.get_barrier_semaphore()

    @pl.when(has_prev)
    def _():
        pl.semaphore_signal(barrier, inc=1, device_id={"layer": l - 1}, device_id_type=MESH)

    @pl.when(has_next)
    def _():
        pl.semaphore_signal(barrier, inc=1, device_id={"layer": l + 1}, device_id_type=MESH)

    @pl.when(to_second)
    def _():
        pl.semaphore_signal(barrier, inc=1, device_id={"layer": l - 2}, device_id_type=MESH)

    @pl.when(from_second)
    def _():
        pl.semaphore_signal(barrier, inc=1, device_id={"layer": l + 2}, device_id_type=MESH)

    pl.semaphore_signal(barrier, inc=1, device_id={"chan": 1 - c}, device_id_type=MESH)
    for k in range(1, dps):
        pl.semaphore_signal(
            barrier, inc=1, device_id={"dp": lax.rem(d + k, dps)}, device_id_type=MESH
        )
    along = (l + layers - 1) // layers + (2 * layers - 2 - l) // layers
    second = (l + layers - 2) // layers + (behind + layers - 2) // layers
    pl.semaphore_wait(barrier, dps + along + lax.rem(behind, 2) * second)

    def guess_copy(n):
        return pltpu.make_async_remote_copy(
            src_ref=guess_hbm.at[n], dst_ref=gbuf.at[n],
            send_sem=gsend.at[n], recv_sem=grecv.at[n],
            device_id={"layer": l - 1}, device_id_type=MESH,
        )

    def corr_copy(n, source):
        return pltpu.make_async_remote_copy(
            src_ref=source.at[n], dst_ref=rbuf.at[n],
            send_sem=csend.at[n], recv_sem=crecv.at[n],
            device_id={"layer": l - 1}, device_id_type=MESH,
        )

    def second_copy(n):
        return pltpu.make_async_remote_copy(
            src_ref=kout.at[n], dst_ref=kbuf.at[n],
            send_sem=ksend.at[n], recv_sem=krecv.at[n],
            device_id={"layer": l - 2}, device_id_type=MESH,
        )

    rates_copy = pltpu.make_async_remote_copy(
        src_ref=rates_ref, dst_ref=rnext, send_sem=rsend.at[0], recv_sem=rrecv.at[0],
        device_id={"layer": l - 1}, device_id_type=MESH,
    )

    early = min(2, samples)

    @pl.when(has_prev)
    def _():
        for n in range(early):
            guess_copy(n).start()
        rates_copy.start()

    @pl.when(has_prev & has_next)
    def _():
        for n in range(early, samples):
            guess_copy(n).start()

    shifts[:, 0] = jnp.zeros((samples,) + shifts.shape[2:], shifts.dtype)
    shifts[:, side + 1] = jnp.zeros((samples,) + shifts.shape[2:], shifts.dtype)
    for load in loads:
        load.wait()
    for slot in range(slots):
        for tap in range(9):
            wt[slot, tap * chan:(tap + 1) * chan] = w[slot, tap].T
    for slot in range(slots):
        for n in range(samples):
            at[slot, :, n * cells:(n + 1) * cells] = acts[slot, n].reshape(cells, chan).T

    @pl.when(jnp.logical_not(from_second))
    def _():
        kbuf[...] = jnp.zeros(kbuf.shape, kbuf.dtype)

    @pl.when(jnp.logical_not(has_next))
    def _():
        rnext[...] = jnp.zeros(rnext.shape, rnext.dtype)

    @pl.when(has_next)
    def _():
        rates_copy.wait_recv()

    count = count_ref[0]
    coefs = [jnp.where(slot < count, STEP, 0.0).astype(jnp.float32) for slot in range(slots)]

    def spread(lo, number):
        rows = number * cells
        value = state[lo * cells:lo * cells + rows]
        place = lax.broadcasted_iota(jnp.int32, (rows, chan), 0) % side
        right = jnp.where(place == side - 1, 0.0, pltpu.roll(value, rows - 1, 0))
        left = jnp.where(place == 0, 0.0, pltpu.roll(value, 1, 0))
        for at_lane, piece in enumerate((right, value, left)):
            shifts[lo:lo + number, 1:side + 1, :, at_lane * chan:(at_lane + 1) * chan] = (
                piece.astype(jnp.bfloat16).reshape(number, side, side, chan)
            )

    def moved(lo, number, row):
        first = 2 - row
        return shifts[lo:lo + number, first:first + side].reshape(number * cells, 3 * chan)

    def advance(lo, number, slot):
        rows = slice(lo * cells, (lo + number) * cells)
        back = None
        for row in range(3):
            term = jnp.dot(
                moved(lo, number, row), wt[slot, row * 3 * chan:(row + 1) * 3 * chan],
                preferred_element_type=jnp.float32,
            )
            back = term if back is None else back + term
        a = acts[slot, lo:lo + number].reshape(number * cells, chan).astype(jnp.float32)
        state[rows] = state[rows] + coefs[slot] * (1.0 - a * a) * back

    def gradient(lo, number, slot, add):
        for row in range(3):
            value = coefs[slot] * jnp.dot(
                at[slot, :, lo * cells:(lo + number) * cells], moved(lo, number, row),
                preferred_element_type=jnp.float32,
            )
            for col in range(3):
                start = (row * 3 + col) * chan
                tile = value[:, col * chan:(col + 1) * chan]
                done = 0
                while done < chan:
                    which, place = divmod(start + done, half)
                    size = min(chan - done, half - place)
                    piece = tile[done:done + size]
                    if add:
                        piece = piece + grad[slot, which, place:place + size]
                    grad[slot, which, place:place + size] = piece
                    done += size

    def settle(n):
        @pl.when(jnp.logical_not(has_next))
        def _():
            rbuf[n] = gbuf[n]

        @pl.when(has_next)
        def _():
            corr_copy(n, cbuf).wait_recv()

        @pl.when(from_second)
        def _():
            second_copy(n).wait_recv()

        above = rbuf[n].astype(jnp.float32).reshape(cells, chan)
        term = rnext[...] * kbuf[n].astype(jnp.float32).reshape(cells, chan)
        above = above + jnp.where(from_second, 1.0, 0.0).astype(jnp.float32) * term
        later = above - gbuf[n].astype(jnp.float32).reshape(cells, chan)
        whole = prop_of(n) + rates_ref[...] * later
        cbuf[n] = whole.astype(jnp.bfloat16).reshape(side, side, chan)
        alone = whole - own[n].astype(jnp.float32).reshape(cells, chan)
        kout[n] = alone.astype(jnp.bfloat16).reshape(side, side, chan)

        @pl.when(to_second)
        def _():
            second_copy(n).start()

        @pl.when(has_prev & odd)
        def _():
            corr_copy(n, cbuf).start()

        start[n * cells:(n + 1) * cells] = above

    def prop_of(n):
        return state[n * cells:(n + 1) * cells]

    @pl.when(jnp.logical_not(has_next))
    def _():
        load_term.wait()

    for n in range(samples):
        @pl.when(has_next)
        def _():
            guess_copy(n).wait_recv()

        state[n * cells:(n + 1) * cells] = gbuf[n].astype(jnp.float32).reshape(cells, chan)
        for slot in reversed(range(slots)):
            spread(n, 1)
            advance(n, 1, slot)
        pbuf[n] = prop_of(n).astype(jnp.bfloat16).reshape(side, side, chan)

        @pl.when(has_prev & jnp.logical_not(odd))
        def _():
            corr_copy(n, pbuf).start()

        if n + early < samples:
            @pl.when(has_prev & jnp.logical_not(has_next))
            def _():
                guess_copy(n + early).start()

        if n < samples - 1:
            for m in range(n + 1):
                @pl.when(behind == n - m)
                def _():
                    settle(m)

    top = slots - 1
    for n in range(samples):
        @pl.when(behind >= samples - 1 - n)
        def _():
            settle(n)

        state[n * cells:(n + 1) * cells] = (
            start[n * cells:(n + 1) * cells].astype(jnp.bfloat16).astype(jnp.float32)
        )
        spread(n, 1)
        gradient(n, 1, top, n > 0)
        advance(n, 1, top)

    out_corr = pltpu.make_async_copy(cbuf, corr_hbm, out_sem.at[0, 0])
    out_corr.start()

    def partner_copy(slot):
        return pltpu.make_async_remote_copy(
            src_ref=grad.at[slot, 1 - c], dst_ref=part.at[slot],
            send_sem=psend.at[slot], recv_sem=precv.at[slot],
            device_id={"chan": 1 - c}, device_id_type=MESH,
        )

    def peer_copy(slot, source, target):
        return pltpu.make_async_remote_copy(
            src_ref=xbuf.at[source, slot], dst_ref=xbuf.at[source, slot],
            send_sem=xsend.at[slot, target], recv_sem=xrecv.at[slot, source],
            device_id={"dp": target}, device_id_type=MESH,
        )

    def final_copy(slot, which):
        return pltpu.make_async_remote_copy(
            src_ref=fin.at[slot, which], dst_ref=fin.at[slot, which],
            send_sem=fsend.at[slot], recv_sem=frecv.at[slot],
            device_id={"chan": 1 - c}, device_id_type=MESH,
        )

    def out_copy(slot, which, sem):
        return pltpu.make_async_copy(
            fin.at[slot, which], grads_hbm.at[slot, which], out_sem.at[sem, slot]
        )

    def chip_sum(slot):
        partner_copy(slot).wait_recv()
        xbuf[d, slot] = (grad[slot, c] + part[slot]).astype(jnp.bfloat16)
        for k in range(1, dps):
            peer_copy(slot, d, lax.rem(d + k, dps)).start()

    def finish(slot):
        for k in range(1, dps):
            peer_copy(slot, lax.rem(d + k, dps), lax.rem(d + k, dps)).wait_recv()
        total = xbuf[0, slot].astype(jnp.float32)
        for e in range(1, dps):
            total = total + xbuf[e, slot].astype(jnp.float32)
        fin[slot, c] = total.astype(jnp.bfloat16)
        final_copy(slot, c).start()
        out_copy(slot, c, 1).start()

    def collect(slot):
        final_copy(slot, 1 - c).wait_recv()
        out_copy(slot, 1 - c, 2).start()

    partner_copy(top).start()
    for slot in reversed(range(top)):
        spread(0, samples)
        gradient(0, samples, slot, False)
        partner_copy(slot).start()
        chip_sum(slot + 1)
        if slot:
            advance(0, samples, slot)
    chip_sum(0)
    for slot in reversed(range(slots)):
        finish(slot)
        if slot < top:
            collect(slot + 1)
    collect(0)

    @pl.when(has_prev)
    def _():
        for n in range(samples):
            guess_copy(n).wait_send()
            corr_copy(n, cbuf).wait_send()
        rates_copy.wait_send()

    @pl.when(to_second)
    def _():
        for n in range(samples):
            second_copy(n).wait_send()

    out_corr.wait()
    for slot in range(slots):
        partner_copy(slot).wait_send()
        for k in range(1, dps):
            peer_copy(slot, d, lax.rem(d + k, dps)).wait_send()
        final_copy(slot, c).wait_send()
        out_copy(slot, c, 1).wait()
        out_copy(slot, 1 - c, 2).wait()


def per_device(sizes, activations, weights, guesses, terminal, coarse_rates, block_layers):
    _, slots, samples, side, _, chan = activations.shape
    taps = weights.shape[2]
    layers, dps, chans = sizes
    half = taps * chan // 2
    cells = side * side
    bf, f32 = jnp.bfloat16, jnp.float32
    anywhere = pl.BlockSpec(memory_space=pl.ANY)
    dma = pltpu.SemaphoreType.DMA
    flops = 2 * samples * cells * chan * chan * taps * slots * 3
    corrected, grads = pl.pallas_call(
        functools.partial(kernel, sizes),
        out_shape=(
            jax.ShapeDtypeStruct((samples, side, side, chan), bf),
            jax.ShapeDtypeStruct((slots, 2, half, chan), bf),
        ),
        in_specs=[anywhere] * 4
        + [pl.BlockSpec(memory_space=pltpu.VMEM), pl.BlockSpec(memory_space=pltpu.SMEM)],
        out_specs=(anywhere, anywhere),
        scratch_shapes=[
            pltpu.VMEM((slots, samples, side, side, chan), bf),
            pltpu.VMEM((slots, taps, chan, chan), bf),
            pltpu.VMEM((slots, taps * chan, chan), bf),
            pltpu.VMEM((slots, chan, samples * cells), bf),
            pltpu.VMEM((samples, side, side, chan), bf),
            pltpu.VMEM((samples, side, side, chan), bf),
            pltpu.VMEM((samples, side, side, chan), bf),
            pltpu.VMEM((samples, side, side, chan), bf),
            pltpu.VMEM((samples, side, side, chan), bf),
            pltpu.VMEM((samples, side, side, chan), bf),
            pltpu.VMEM((samples, side, side, chan), bf),
            pltpu.VMEM((1, chan), f32),
            pltpu.VMEM((samples * cells, chan), f32),
            pltpu.VMEM((samples * cells, chan), f32),
            pltpu.VMEM((samples, side + 2, side, 3 * chan), bf),
            pltpu.VMEM((slots, 2, half, chan), f32),
            pltpu.VMEM((slots, half, chan), f32),
            pltpu.VMEM((dps, slots, half, chan), bf),
            pltpu.VMEM((slots, 2, half, chan), bf),
            dma((4,)),
            dma((samples,)), dma((samples,)), dma((samples,)), dma((samples,)),
            dma((samples,)), dma((samples,)), dma((1,)), dma((1,)),
            dma((slots,)), dma((slots,)),
            dma((slots, dps)), dma((slots, dps)),
            dma((slots,)), dma((slots,)),
            dma((3, slots)),
        ],
        compiler_params=pltpu.CompilerParams(
            collective_id=0, has_side_effects=True, vmem_limit_bytes=60 * 1024 * 1024
        ),
        cost_estimate=pl.CostEstimate(flops=flops, bytes_accessed=5_000_000, transcendentals=0),
        name="sweep",
    )(activations[0], weights[0], guesses[0], terminal, coarse_rates, block_layers)
    return corrected[None], grads.reshape(1, slots, taps, chan, chan)


def solution(mesh):
    sizes = (mesh.shape["layer"], mesh.shape["dp"], mesh.shape["chan"])
    batch = ("groups", "dp", "chan")
    in_specs = (
        P("layer", None, batch, None, None, None),
        P("layer", None, None, None, None),
        P("layer", batch, None, None, None),
        P(batch, None, None, None),
        P("layer", None),
        P("layer"),
    )
    out_specs = (
        P("layer", batch, None, None, None),
        P(("groups", "layer"), None, None, None, None),
    )
    return jax.shard_map(
        functools.partial(per_device, sizes),
        mesh=mesh, in_specs=in_specs, out_specs=out_specs, check_vma=False,
    )
```

```python
import functools

import jax
import jax.numpy as jnp
from jax import lax
from jax.experimental import pallas as pl
from jax.experimental.pallas import tpu as pltpu
from jax.sharding import PartitionSpec as P

STEP = 0.25
MESH = pl.DeviceIdType.MESH


def kernel(
    sizes,
    acts_hbm, w_hbm, guess_hbm, term_hbm, rates_ref, count_ref,
    corr_hbm, grads_hbm,
    acts, w, wt, at, gbuf, rbuf, kbuf, cbuf, pbuf, kout, own, rnext, state, start, shifts, grad, part, xbuf, fin,
    local_sem, gsend, grecv, csend, crecv, ksend, krecv, rsend, rrecv, psend, precv, xsend, xrecv, fsend, frecv, out_sem,
):
    layers, dps, chans = sizes
    slots, samples, side, _, chan = acts.shape
    cells = side * side
    l, d, c = lax.axis_index("layer"), lax.axis_index("dp"), lax.axis_index("chan")
    has_next, has_prev = l < layers - 1, l > 0
    half = grad.shape[2]
    behind = layers - 1 - l
    odd = lax.rem(behind, 2) == 1
    to_second = odd & (l > 1)
    from_second = odd & (behind > 1)

    loads = [
        pltpu.make_async_copy(w_hbm, w, local_sem.at[0]),
        pltpu.make_async_copy(acts_hbm, acts, local_sem.at[1]),
        pltpu.make_async_copy(guess_hbm, own, local_sem.at[3]),
    ]
    for load in loads:
        load.start()
    load_term = pltpu.make_async_copy(term_hbm, gbuf, local_sem.at[2])

    @pl.when(jnp.logical_not(has_next))
    def _():
        load_term.start()

    barrier = pltpu.get_barrier_semaphore()

    @pl.when(has_prev)
    def _():
        pl.semaphore_signal(barrier, inc=1, device_id={"layer": l - 1}, device_id_type=MESH)

    @pl.when(has_next)
    def _():
        pl.semaphore_signal(barrier, inc=1, device_id={"layer": l + 1}, device_id_type=MESH)

    @pl.when(to_second)
    def _():
        pl.semaphore_signal(barrier, inc=1, device_id={"layer": l - 2}, device_id_type=MESH)

    @pl.when(from_second)
    def _():
        pl.semaphore_signal(barrier, inc=1, device_id={"layer": l + 2}, device_id_type=MESH)

    pl.semaphore_signal(barrier, inc=1, device_id={"chan": 1 - c}, device_id_type=MESH)
    for k in range(1, dps):
        pl.semaphore_signal(
            barrier, inc=1, device_id={"dp": lax.rem(d + k, dps)}, device_id_type=MESH
        )
    along = (l + layers - 1) // layers + (2 * layers - 2 - l) // layers
    second = (l + layers - 2) // layers + (behind + layers - 2) // layers
    pl.semaphore_wait(barrier, dps + along + lax.rem(behind, 2) * second)

    def guess_copy(n):
        return pltpu.make_async_remote_copy(
            src_ref=guess_hbm.at[n], dst_ref=gbuf.at[n],
            send_sem=gsend.at[n], recv_sem=grecv.at[n],
            device_id={"layer": l - 1}, device_id_type=MESH,
        )

    def corr_copy(n, source):
        return pltpu.make_async_remote_copy(
            src_ref=source.at[n], dst_ref=rbuf.at[n],
            send_sem=csend.at[n], recv_sem=crecv.at[n],
            device_id={"layer": l - 1}, device_id_type=MESH,
        )

    def second_copy(n):
        return pltpu.make_async_remote_copy(
            src_ref=kout.at[n], dst_ref=kbuf.at[n],
            send_sem=ksend.at[n], recv_sem=krecv.at[n],
            device_id={"layer": l - 2}, device_id_type=MESH,
        )

    rates_copy = pltpu.make_async_remote_copy(
        src_ref=rates_ref, dst_ref=rnext, send_sem=rsend.at[0], recv_sem=rrecv.at[0],
        device_id={"layer": l - 1}, device_id_type=MESH,
    )

    early = min(2, samples)

    @pl.when(has_prev)
    def _():
        for n in range(early):
            guess_copy(n).start()
        rates_copy.start()

    @pl.when(has_prev & has_next)
    def _():
        for n in range(early, samples):
            guess_copy(n).start()

    shifts[:, 0] = jnp.zeros((samples,) + shifts.shape[2:], shifts.dtype)
    shifts[:, side + 1] = jnp.zeros((samples,) + shifts.shape[2:], shifts.dtype)
    for load in loads:
        load.wait()
    for slot in range(slots):
        for tap in range(9):
            wt[slot, tap * chan:(tap + 1) * chan] = w[slot, tap].T
    for slot in range(slots):
        for n in range(samples):
            at[slot, :, n * cells:(n + 1) * cells] = acts[slot, n].reshape(cells, chan).T

    @pl.when(jnp.logical_not(from_second))
    def _():
        kbuf[...] = jnp.zeros(kbuf.shape, kbuf.dtype)

    @pl.when(jnp.logical_not(has_next))
    def _():
        rnext[...] = jnp.zeros(rnext.shape, rnext.dtype)

    @pl.when(has_next)
    def _():
        rates_copy.wait_recv()

    count = count_ref[0]
    coefs = [jnp.where(slot < count, STEP, 0.0).astype(jnp.float32) for slot in range(slots)]

    def spread(lo, number):
        rows = number * cells
        value = state[lo * cells:lo * cells + rows]
        place = lax.broadcasted_iota(jnp.int32, (rows, chan), 0) % side
        right = jnp.where(place == side - 1, 0.0, pltpu.roll(value, rows - 1, 0))
        left = jnp.where(place == 0, 0.0, pltpu.roll(value, 1, 0))
        for at_lane, piece in enumerate((right, value, left)):
            shifts[lo:lo + number, 1:side + 1, :, at_lane * chan:(at_lane + 1) * chan] = (
                piece.astype(jnp.bfloat16).reshape(number, side, side, chan)
            )

    def moved(lo, number, row):
        first = 2 - row
        return shifts[lo:lo + number, first:first + side].reshape(number * cells, 3 * chan)

    def advance(lo, number, slot):
        rows = slice(lo * cells, (lo + number) * cells)
        back = None
        for row in range(3):
            term = jnp.dot(
                moved(lo, number, row), wt[slot, row * 3 * chan:(row + 1) * 3 * chan],
                preferred_element_type=jnp.float32,
            )
            back = term if back is None else back + term
        a = acts[slot, lo:lo + number].reshape(number * cells, chan).astype(jnp.float32)
        state[rows] = state[rows] + coefs[slot] * (1.0 - a * a) * back

    def gradient(lo, number, slot, add):
        for row in range(3):
            value = coefs[slot] * jnp.dot(
                at[slot, :, lo * cells:(lo + number) * cells], moved(lo, number, row),
                preferred_element_type=jnp.float32,
            )
            for col in range(3):
                start = (row * 3 + col) * chan
                tile = value[:, col * chan:(col + 1) * chan]
                done = 0
                while done < chan:
                    which, place = divmod(start + done, half)
                    size = min(chan - done, half - place)
                    piece = tile[done:done + size]
                    if add:
                        piece = piece + grad[slot, which, place:place + size]
                    grad[slot, which, place:place + size] = piece
                    done += size

    def settle(n):
        @pl.when(jnp.logical_not(has_next))
        def _():
            rbuf[n] = gbuf[n]

        @pl.when(has_next)
        def _():
            corr_copy(n, cbuf).wait_recv()

        @pl.when(from_second)
        def _():
            second_copy(n).wait_recv()

        above = rbuf[n].astype(jnp.float32).reshape(cells, chan)
        term = rnext[...] * kbuf[n].astype(jnp.float32).reshape(cells, chan)
        above = above + jnp.where(from_second, 1.0, 0.0).astype(jnp.float32) * term
        later = above - gbuf[n].astype(jnp.float32).reshape(cells, chan)
        whole = prop_of(n) + rates_ref[...] * later
        cbuf[n] = whole.astype(jnp.bfloat16).reshape(side, side, chan)
        alone = whole - own[n].astype(jnp.float32).reshape(cells, chan)
        kout[n] = alone.astype(jnp.bfloat16).reshape(side, side, chan)

        @pl.when(to_second)
        def _():
            second_copy(n).start()

        @pl.when(has_prev & odd)
        def _():
            corr_copy(n, cbuf).start()

        start[n * cells:(n + 1) * cells] = above

    def prop_of(n):
        return state[n * cells:(n + 1) * cells]

    @pl.when(jnp.logical_not(has_next))
    def _():
        load_term.wait()

    for n in range(samples):
        @pl.when(has_next)
        def _():
            guess_copy(n).wait_recv()

        state[n * cells:(n + 1) * cells] = gbuf[n].astype(jnp.float32).reshape(cells, chan)
        for slot in reversed(range(slots)):
            spread(n, 1)
            advance(n, 1, slot)
        pbuf[n] = prop_of(n).astype(jnp.bfloat16).reshape(side, side, chan)

        @pl.when(has_prev & jnp.logical_not(odd))
        def _():
            corr_copy(n, pbuf).start()

        if n + early < samples:
            @pl.when(has_prev & jnp.logical_not(has_next))
            def _():
                guess_copy(n + early).start()

        if n < samples - 1:
            for m in range(n + 1):
                @pl.when(behind == n - m)
                def _():
                    settle(m)

    top = slots - 1
    for n in range(samples):
        @pl.when(behind >= samples - 1 - n)
        def _():
            settle(n)

        state[n * cells:(n + 1) * cells] = (
            start[n * cells:(n + 1) * cells].astype(jnp.bfloat16).astype(jnp.float32)
        )
        spread(n, 1)
        gradient(n, 1, top, n > 0)
        advance(n, 1, top)

    out_corr = pltpu.make_async_copy(cbuf, corr_hbm, out_sem.at[0, 0])
    out_corr.start()

    def partner_copy(slot):
        return pltpu.make_async_remote_copy(
            src_ref=grad.at[slot, 1 - c], dst_ref=part.at[slot],
            send_sem=psend.at[slot], recv_sem=precv.at[slot],
            device_id={"chan": 1 - c}, device_id_type=MESH,
        )

    def peer_copy(slot, source, target):
        return pltpu.make_async_remote_copy(
            src_ref=xbuf.at[source, slot], dst_ref=xbuf.at[source, slot],
            send_sem=xsend.at[slot, target], recv_sem=xrecv.at[slot, source],
            device_id={"dp": target}, device_id_type=MESH,
        )

    def final_copy(slot, which):
        return pltpu.make_async_remote_copy(
            src_ref=fin.at[slot, which], dst_ref=fin.at[slot, which],
            send_sem=fsend.at[slot], recv_sem=frecv.at[slot],
            device_id={"chan": 1 - c}, device_id_type=MESH,
        )

    def out_copy(slot, which, sem):
        return pltpu.make_async_copy(
            fin.at[slot, which], grads_hbm.at[slot, which], out_sem.at[sem, slot]
        )

    def chip_sum(slot):
        partner_copy(slot).wait_recv()
        xbuf[d, slot] = (grad[slot, c] + part[slot]).astype(jnp.bfloat16)
        for k in range(1, dps):
            peer_copy(slot, d, lax.rem(d + k, dps)).start()

    def finish(slot):
        for k in range(1, dps):
            peer_copy(slot, lax.rem(d + k, dps), lax.rem(d + k, dps)).wait_recv()
        total = xbuf[0, slot].astype(jnp.float32)
        for e in range(1, dps):
            total = total + xbuf[e, slot].astype(jnp.float32)
        fin[slot, c] = total.astype(jnp.bfloat16)
        final_copy(slot, c).start()
        out_copy(slot, c, 1).start()

    def collect(slot):
        final_copy(slot, 1 - c).wait_recv()
        out_copy(slot, 1 - c, 2).start()

    partner_copy(top).start()
    for slot in reversed(range(top)):
        spread(0, samples)
        gradient(0, samples, slot, False)
        partner_copy(slot).start()
        chip_sum(slot + 1)
        if slot:
            advance(0, samples, slot)
    chip_sum(0)
    for slot in reversed(range(slots)):
        finish(slot)
        if slot < top:
            collect(slot + 1)
    collect(0)

    @pl.when(has_prev)
    def _():
        for n in range(samples):
            guess_copy(n).wait_send()
            corr_copy(n, cbuf).wait_send()
        rates_copy.wait_send()

    @pl.when(to_second)
    def _():
        for n in range(samples):
            second_copy(n).wait_send()

    out_corr.wait()
    for slot in range(slots):
        partner_copy(slot).wait_send()
        for k in range(1, dps):
            peer_copy(slot, d, lax.rem(d + k, dps)).wait_send()
        final_copy(slot, c).wait_send()
        out_copy(slot, c, 1).wait()
        out_copy(slot, 1 - c, 2).wait()


def per_device(sizes, activations, weights, guesses, terminal, coarse_rates, block_layers):
    _, slots, samples, side, _, chan = activations.shape
    taps = weights.shape[2]
    layers, dps, chans = sizes
    half = taps * chan // 2
    cells = side * side
    bf, f32 = jnp.bfloat16, jnp.float32
    anywhere = pl.BlockSpec(memory_space=pl.ANY)
    dma = pltpu.SemaphoreType.DMA
    flops = 2 * samples * cells * chan * chan * taps * slots * 3
    corrected, grads = pl.pallas_call(
        functools.partial(kernel, sizes),
        out_shape=(
            jax.ShapeDtypeStruct((samples, side, side, chan), bf),
            jax.ShapeDtypeStruct((slots, 2, half, chan), bf),
        ),
        in_specs=[pl.BlockSpec(memory_space=pltpu.HBM)] * 4
        + [pl.BlockSpec(memory_space=pltpu.VMEM), pl.BlockSpec(memory_space=pltpu.SMEM)],
        out_specs=(anywhere, anywhere),
        scratch_shapes=[
            pltpu.VMEM((slots, samples, side, side, chan), bf),
            pltpu.VMEM((slots, taps, chan, chan), bf),
            pltpu.VMEM((slots, taps * chan, chan), bf),
            pltpu.VMEM((slots, chan, samples * cells), bf),
            pltpu.VMEM((samples, side, side, chan), bf),
            pltpu.VMEM((samples, side, side, chan), bf),
            pltpu.VMEM((samples, side, side, chan), bf),
            pltpu.VMEM((samples, side, side, chan), bf),
            pltpu.VMEM((samples, side, side, chan), bf),
            pltpu.VMEM((samples, side, side, chan), bf),
            pltpu.VMEM((samples, side, side, chan), bf),
            pltpu.VMEM((1, chan), f32),
            pltpu.VMEM((samples * cells, chan), f32),
            pltpu.VMEM((samples * cells, chan), f32),
            pltpu.VMEM((samples, side + 2, side, 3 * chan), bf),
            pltpu.VMEM((slots, 2, half, chan), f32),
            pltpu.VMEM((slots, half, chan), f32),
            pltpu.VMEM((dps, slots, half, chan), bf),
            pltpu.VMEM((slots, 2, half, chan), bf),
            dma((4,)),
            dma((samples,)), dma((samples,)), dma((samples,)), dma((samples,)),
            dma((samples,)), dma((samples,)), dma((1,)), dma((1,)),
            dma((slots,)), dma((slots,)),
            dma((slots, dps)), dma((slots, dps)),
            dma((slots,)), dma((slots,)),
            dma((3, slots)),
        ],
        compiler_params=pltpu.CompilerParams(
            collective_id=0, has_side_effects=True, vmem_limit_bytes=40 * 1024 * 1024
        ),
        cost_estimate=pl.CostEstimate(flops=flops, bytes_accessed=5_000_000, transcendentals=0),
        name="sweep",
    )(*[pltpu.with_memory_space_constraint(v, pltpu.HBM) for v in (activations[0], weights[0], guesses[0], terminal)], coarse_rates, block_layers)
    return corrected[None], grads.reshape(1, slots, taps, chan, chan)


def solution(mesh):
    sizes = (mesh.shape["layer"], mesh.shape["dp"], mesh.shape["chan"])
    batch = ("groups", "dp", "chan")
    in_specs = (
        P("layer", None, batch, None, None, None),
        P("layer", None, None, None, None),
        P("layer", batch, None, None, None),
        P(batch, None, None, None),
        P("layer", None),
        P("layer"),
    )
    out_specs = (
        P("layer", batch, None, None, None),
        P(("groups", "layer"), None, None, None, None),
    )
    return jax.shard_map(
        functools.partial(per_device, sizes),
        mesh=mesh, in_specs=in_specs, out_specs=out_specs, check_vma=False,
    )
```

```python
import functools

import jax
import jax.numpy as jnp
from jax import lax
from jax.experimental import pallas as pl
from jax.experimental.pallas import tpu as pltpu
from jax.sharding import PartitionSpec as P

STEP = 0.25
MESH = pl.DeviceIdType.MESH


def kernel(
    sizes,
    acts_hbm, w_hbm, guess_hbm, term_hbm, rates_hbm, count_ref,
    corr_hbm, grads_hbm,
    acts, w, wt, at, gbuf, rbuf, kbuf, cbuf, pbuf, kout, own, rates_ref, rnext, state, start, shifts, grad, part, xbuf, fin,
    local_sem, gsend, grecv, csend, crecv, ksend, krecv, rsend, rrecv, psend, precv, xsend, xrecv, fsend, frecv, out_sem,
):
    layers, dps, chans = sizes
    slots, samples, side, _, chan = acts.shape
    cells = side * side
    l, d, c = lax.axis_index("layer"), lax.axis_index("dp"), lax.axis_index("chan")
    has_next, has_prev = l < layers - 1, l > 0
    half = grad.shape[2]
    behind = layers - 1 - l
    odd = lax.rem(behind, 2) == 1
    to_second = odd & (l > 1)
    from_second = odd & (behind > 1)

    loads = [
        pltpu.make_async_copy(w_hbm, w, local_sem.at[0]),
        pltpu.make_async_copy(acts_hbm, acts, local_sem.at[1]),
        pltpu.make_async_copy(guess_hbm, own, local_sem.at[3]),
        pltpu.make_async_copy(rates_hbm, rates_ref, local_sem.at[4]),
    ]
    for load in loads:
        load.start()
    load_term = pltpu.make_async_copy(term_hbm, gbuf, local_sem.at[2])

    @pl.when(jnp.logical_not(has_next))
    def _():
        load_term.start()

    barrier = pltpu.get_barrier_semaphore()

    @pl.when(has_prev)
    def _():
        pl.semaphore_signal(barrier, inc=1, device_id={"layer": l - 1}, device_id_type=MESH)

    @pl.when(has_next)
    def _():
        pl.semaphore_signal(barrier, inc=1, device_id={"layer": l + 1}, device_id_type=MESH)

    @pl.when(to_second)
    def _():
        pl.semaphore_signal(barrier, inc=1, device_id={"layer": l - 2}, device_id_type=MESH)

    @pl.when(from_second)
    def _():
        pl.semaphore_signal(barrier, inc=1, device_id={"layer": l + 2}, device_id_type=MESH)

    pl.semaphore_signal(barrier, inc=1, device_id={"chan": 1 - c}, device_id_type=MESH)
    for k in range(1, dps):
        pl.semaphore_signal(
            barrier, inc=1, device_id={"dp": lax.rem(d + k, dps)}, device_id_type=MESH
        )
    along = (l + layers - 1) // layers + (2 * layers - 2 - l) // layers
    second = (l + layers - 2) // layers + (behind + layers - 2) // layers
    pl.semaphore_wait(barrier, dps + along + lax.rem(behind, 2) * second)

    def guess_copy(n):
        return pltpu.make_async_remote_copy(
            src_ref=guess_hbm.at[n], dst_ref=gbuf.at[n],
            send_sem=gsend.at[n], recv_sem=grecv.at[n],
            device_id={"layer": l - 1}, device_id_type=MESH,
        )

    def corr_copy(n, source):
        return pltpu.make_async_remote_copy(
            src_ref=source.at[n], dst_ref=rbuf.at[n],
            send_sem=csend.at[n], recv_sem=crecv.at[n],
            device_id={"layer": l - 1}, device_id_type=MESH,
        )

    def second_copy(n):
        return pltpu.make_async_remote_copy(
            src_ref=kout.at[n], dst_ref=kbuf.at[n],
            send_sem=ksend.at[n], recv_sem=krecv.at[n],
            device_id={"layer": l - 2}, device_id_type=MESH,
        )

    rates_copy = pltpu.make_async_remote_copy(
        src_ref=rates_ref, dst_ref=rnext, send_sem=rsend.at[0], recv_sem=rrecv.at[0],
        device_id={"layer": l - 1}, device_id_type=MESH,
    )

    early = min(2, samples)

    @pl.when(has_prev)
    def _():
        for n in range(early):
            guess_copy(n).start()

    @pl.when(has_prev & has_next)
    def _():
        for n in range(early, samples):
            guess_copy(n).start()

    shifts[:, 0] = jnp.zeros((samples,) + shifts.shape[2:], shifts.dtype)
    shifts[:, side + 1] = jnp.zeros((samples,) + shifts.shape[2:], shifts.dtype)
    for load in loads:
        load.wait()

    @pl.when(has_prev)
    def _():
        rates_copy.start()

    for slot in range(slots):
        for tap in range(9):
            wt[slot, tap * chan:(tap + 1) * chan] = w[slot, tap].T
    for slot in range(slots):
        for n in range(samples):
            at[slot, :, n * cells:(n + 1) * cells] = acts[slot, n].reshape(cells, chan).T

    @pl.when(jnp.logical_not(from_second))
    def _():
        kbuf[...] = jnp.zeros(kbuf.shape, kbuf.dtype)

    @pl.when(jnp.logical_not(has_next))
    def _():
        rnext[...] = jnp.zeros(rnext.shape, rnext.dtype)

    @pl.when(has_next)
    def _():
        rates_copy.wait_recv()

    count = count_ref[0]
    coefs = [jnp.where(slot < count, STEP, 0.0).astype(jnp.float32) for slot in range(slots)]

    def spread(lo, number):
        rows = number * cells
        value = state[lo * cells:lo * cells + rows]
        place = lax.broadcasted_iota(jnp.int32, (rows, chan), 0) % side
        right = jnp.where(place == side - 1, 0.0, pltpu.roll(value, rows - 1, 0))
        left = jnp.where(place == 0, 0.0, pltpu.roll(value, 1, 0))
        for at_lane, piece in enumerate((right, value, left)):
            shifts[lo:lo + number, 1:side + 1, :, at_lane * chan:(at_lane + 1) * chan] = (
                piece.astype(jnp.bfloat16).reshape(number, side, side, chan)
            )

    def moved(lo, number, row):
        first = 2 - row
        return shifts[lo:lo + number, first:first + side].reshape(number * cells, 3 * chan)

    def advance(lo, number, slot):
        rows = slice(lo * cells, (lo + number) * cells)
        back = None
        for row in range(3):
            term = jnp.dot(
                moved(lo, number, row), wt[slot, row * 3 * chan:(row + 1) * 3 * chan],
                preferred_element_type=jnp.float32,
            )
            back = term if back is None else back + term
        a = acts[slot, lo:lo + number].reshape(number * cells, chan).astype(jnp.float32)
        state[rows] = state[rows] + coefs[slot] * (1.0 - a * a) * back

    def gradient(lo, number, slot, add):
        for row in range(3):
            value = coefs[slot] * jnp.dot(
                at[slot, :, lo * cells:(lo + number) * cells], moved(lo, number, row),
                preferred_element_type=jnp.float32,
            )
            for col in range(3):
                start = (row * 3 + col) * chan
                tile = value[:, col * chan:(col + 1) * chan]
                done = 0
                while done < chan:
                    which, place = divmod(start + done, half)
                    size = min(chan - done, half - place)
                    piece = tile[done:done + size]
                    if add:
                        piece = piece + grad[slot, which, place:place + size]
                    grad[slot, which, place:place + size] = piece
                    done += size

    def skips(n):
        return n >= 0

    def settle(n):
        @pl.when(jnp.logical_not(has_next))
        def _():
            rbuf[n] = gbuf[n]

        @pl.when(has_next)
        def _():
            corr_copy(n, cbuf).wait_recv()

        above = rbuf[n].astype(jnp.float32).reshape(cells, chan)
        if skips(n):
            @pl.when(from_second)
            def _():
                second_copy(n).wait_recv()

            term = rnext[...] * kbuf[n].astype(jnp.float32).reshape(cells, chan)
            above = above + jnp.where(from_second, 1.0, 0.0).astype(jnp.float32) * term
        later = above - gbuf[n].astype(jnp.float32).reshape(cells, chan)
        whole = prop_of(n) + rates_ref[...] * later
        cbuf[n] = whole.astype(jnp.bfloat16).reshape(side, side, chan)
        if skips(n):
            alone = whole - own[n].astype(jnp.float32).reshape(cells, chan)
            kout[n] = alone.astype(jnp.bfloat16).reshape(side, side, chan)

            @pl.when(to_second)
            def _():
                second_copy(n).start()

        @pl.when(has_prev & odd if skips(n) else has_prev)
        def _():
            corr_copy(n, cbuf).start()

        start[n * cells:(n + 1) * cells] = above

    def prop_of(n):
        return state[n * cells:(n + 1) * cells]

    @pl.when(jnp.logical_not(has_next))
    def _():
        load_term.wait()

    for n in range(samples):
        @pl.when(has_next)
        def _():
            guess_copy(n).wait_recv()

        state[n * cells:(n + 1) * cells] = gbuf[n].astype(jnp.float32).reshape(cells, chan)
        for slot in reversed(range(slots)):
            spread(n, 1)
            advance(n, 1, slot)
        if skips(n):
            pbuf[n] = prop_of(n).astype(jnp.bfloat16).reshape(side, side, chan)

            @pl.when(has_prev & jnp.logical_not(odd))
            def _():
                corr_copy(n, pbuf).start()

        if n + early < samples:
            @pl.when(has_prev & jnp.logical_not(has_next))
            def _():
                guess_copy(n + early).start()

        if n < samples - 1:
            for m in range(n + 1):
                @pl.when(behind == n - m)
                def _():
                    settle(m)

    def partner_copy(slot):
        return pltpu.make_async_remote_copy(
            src_ref=grad.at[slot, 1 - c], dst_ref=part.at[slot],
            send_sem=psend.at[slot], recv_sem=precv.at[slot],
            device_id={"chan": 1 - c}, device_id_type=MESH,
        )

    top = slots - 1
    for n in range(samples):
        @pl.when(behind >= samples - 1 - n)
        def _():
            settle(n)

        state[n * cells:(n + 1) * cells] = (
            start[n * cells:(n + 1) * cells].astype(jnp.bfloat16).astype(jnp.float32)
        )
        spread(n, 1)
        gradient(n, 1, top, n > 0)
        if n == samples - 1:
            partner_copy(top).start()
        advance(n, 1, top)

    out_corr = pltpu.make_async_copy(cbuf, corr_hbm, out_sem.at[0, 0])
    out_corr.start()

    pieces = xsend.shape[1]
    size = half // pieces

    def rows_of(piece):
        return pl.ds(piece * size, size)

    def peer_copy(slot, piece, source, target):
        return pltpu.make_async_remote_copy(
            src_ref=xbuf.at[source, slot, rows_of(piece)],
            dst_ref=xbuf.at[source, slot, rows_of(piece)],
            send_sem=xsend.at[slot, piece, target], recv_sem=xrecv.at[slot, piece, source],
            device_id={"dp": target}, device_id_type=MESH,
        )

    def final_copy(slot, piece, which):
        return pltpu.make_async_remote_copy(
            src_ref=fin.at[slot, which, rows_of(piece)],
            dst_ref=grads_hbm.at[slot, which, rows_of(piece)],
            send_sem=fsend.at[slot, piece], recv_sem=frecv.at[slot, piece],
            device_id={"chan": 1 - c}, device_id_type=MESH,
        )

    def out_copy(slot, which, sem):
        return pltpu.make_async_copy(
            fin.at[slot, which], grads_hbm.at[slot, which], out_sem.at[sem, slot]
        )

    def chip_sum(slot):
        partner_copy(slot).wait_recv()
        for piece in range(pieces):
            rows = rows_of(piece)
            xbuf[d, slot, rows] = (grad[slot, c, rows] + part[slot, rows]).astype(jnp.bfloat16)
            for k in range(1, dps):
                peer_copy(slot, piece, d, lax.rem(d + k, dps)).start()

    def finish(slot):
        for piece in range(pieces):
            rows = rows_of(piece)
            for k in range(1, dps):
                peer = lax.rem(d + k, dps)
                peer_copy(slot, piece, peer, peer).wait_recv()
            total = xbuf[0, slot, rows].astype(jnp.float32)
            for e in range(1, dps):
                total = total + xbuf[e, slot, rows].astype(jnp.float32)
            fin[slot, c, rows] = total.astype(jnp.bfloat16)
            final_copy(slot, piece, c).start()
        out_copy(slot, c, 1).start()

    def collect(slot):
        for piece in range(pieces):
            final_copy(slot, piece, 1 - c).wait_recv()

    for slot in reversed(range(top)):
        spread(0, samples)
        chip_sum(slot + 1)
        gradient(0, samples, slot, False)
        partner_copy(slot).start()
        if slot:
            advance(0, samples, slot)
    chip_sum(0)
    for slot in reversed(range(slots)):
        finish(slot)
        if slot < top:
            collect(slot + 1)
    collect(0)

    @pl.when(has_prev)
    def _():
        for n in range(samples):
            guess_copy(n).wait_send()
            corr_copy(n, cbuf).wait_send()
        rates_copy.wait_send()

    @pl.when(to_second)
    def _():
        for n in range(samples):
            if skips(n):
                second_copy(n).wait_send()

    out_corr.wait()
    for slot in range(slots):
        partner_copy(slot).wait_send()
        for piece in range(pieces):
            for k in range(1, dps):
                peer_copy(slot, piece, d, lax.rem(d + k, dps)).wait_send()
            final_copy(slot, piece, c).wait_send()
        out_copy(slot, c, 1).wait()


def per_device(sizes, activations, weights, guesses, terminal, coarse_rates, block_layers):
    _, slots, samples, side, _, chan = activations.shape
    taps = weights.shape[2]
    layers, dps, chans = sizes
    half = taps * chan // 2
    cells = side * side
    bf, f32 = jnp.bfloat16, jnp.float32
    anywhere = pl.BlockSpec(memory_space=pl.ANY)
    dma = pltpu.SemaphoreType.DMA
    flops = 2 * samples * cells * chan * chan * taps * slots * 3
    corrected, grads = pl.pallas_call(
        functools.partial(kernel, sizes),
        out_shape=(
            jax.ShapeDtypeStruct((samples, side, side, chan), bf),
            jax.ShapeDtypeStruct((slots, 2, half, chan), bf),
        ),
        in_specs=[pl.BlockSpec(memory_space=pltpu.HBM)] * 5 + [pl.BlockSpec(memory_space=pltpu.SMEM)],
        out_specs=(anywhere, anywhere),
        scratch_shapes=[
            pltpu.VMEM((slots, samples, side, side, chan), bf),
            pltpu.VMEM((slots, taps, chan, chan), bf),
            pltpu.VMEM((slots, taps * chan, chan), bf),
            pltpu.VMEM((slots, chan, samples * cells), bf),
            pltpu.VMEM((samples, side, side, chan), bf),
            pltpu.VMEM((samples, side, side, chan), bf),
            pltpu.VMEM((samples, side, side, chan), bf),
            pltpu.VMEM((samples, side, side, chan), bf),
            pltpu.VMEM((samples, side, side, chan), bf),
            pltpu.VMEM((samples, side, side, chan), bf),
            pltpu.VMEM((samples, side, side, chan), bf),
            pltpu.VMEM((1, chan), f32),
            pltpu.VMEM((1, chan), f32),
            pltpu.VMEM((samples * cells, chan), f32),
            pltpu.VMEM((samples * cells, chan), f32),
            pltpu.VMEM((samples, side + 2, side, 3 * chan), bf),
            pltpu.VMEM((slots, 2, half, chan), f32),
            pltpu.VMEM((slots, half, chan), f32),
            pltpu.VMEM((dps, slots, half, chan), bf),
            pltpu.VMEM((slots, 2, half, chan), bf),
            dma((5,)),
            dma((samples,)), dma((samples,)), dma((samples,)), dma((samples,)),
            dma((samples,)), dma((samples,)), dma((1,)), dma((1,)),
            dma((slots,)), dma((slots,)),
            dma((slots, 2, dps)), dma((slots, 2, dps)),
            dma((slots, 2)), dma((slots, 2)),
            dma((3, slots)),
        ],
        compiler_params=pltpu.CompilerParams(
            collective_id=0, has_side_effects=True, vmem_limit_bytes=40 * 1024 * 1024
        ),
        cost_estimate=pl.CostEstimate(flops=flops, bytes_accessed=5_000_000, transcendentals=0),
        name="sweep",
    )(*[pltpu.with_memory_space_constraint(v, pltpu.HBM) for v in (activations[0], weights[0], guesses[0], terminal, coarse_rates)], block_layers)
    return corrected[None], grads.reshape(1, slots, taps, chan, chan)


def solution(mesh):
    sizes = (mesh.shape["layer"], mesh.shape["dp"], mesh.shape["chan"])
    batch = ("groups", "dp", "chan")
    in_specs = (
        P("layer", None, batch, None, None, None),
        P("layer", None, None, None, None),
        P("layer", batch, None, None, None),
        P(batch, None, None, None),
        P("layer", None),
        P("layer"),
    )
    out_specs = (
        P("layer", batch, None, None, None),
        P(("groups", "layer"), None, None, None, None),
    )
    return jax.shard_map(
        functools.partial(per_device, sizes),
        mesh=mesh, in_specs=in_specs, out_specs=out_specs, check_vma=False,
    )
```
